256 devices in a mesh: aux: 32 (over z_hi, x, core), row: 8 (over z_lo, y).
Axes of the slice: x: 4, y: 4, z: 8 (z_hi: 4, z_lo: 2; z = z_hi * 2 + z_lo), core: 2. Of those that a mesh axis runs over, the one named last changes fastest.
Arguments:
- integrals: bfloat16 [128, 1024, 8000], P('aux', 'row'), may hold values from -0.71875 to 0.71875
- block_mask: int32 [32, 16, 16], P('aux', 'row'), may hold values 0 or 1
- coefficients: bfloat16 [8000, 256], P('aux'), may hold values from -0.0625 to 0.0625
- occ_index: int32 [64], replicated, may hold values from 0 to 255
Outputs:
- exchange: float32 [1024, 384], P(('row', 'aux'))
The draws below stay inside these ranges and needn't reach their ends.
All inputs are finite; a program needn't handle non-finite values. No bound on the sum of `block_mask` on one device may be relied on, other than what follows from the above.
Results may differ from the reference program's by a relative error of at most 0.0011.
Values may be sent and summed in bfloat16 or wider, within the bound.
No kernel may reach another device: no remote copies, remote signals or barrier semaphores. Data moves between devices by JAX's collectives and lax.ppermute only.
A program may use at most 128 MiB of HBM per device.

```python
import jax
import jax.numpy as jnp
from jax import lax

BASIS = 8000
COL_BLK = 500
OCC = 256
OCCB = 64
BANDS = 3
P_DEV = 4
ROW_DEV = 128
ROW_BLK = 64
AUX = 128
AUXB = 32
ROWS = 1024
ROWB = 16
COLB = 16
N_ROW = 8


def set_ends(values, rng, smallest, largest):
    longest = values.shape.index(max(values.shape))
    spots = []
    for shift in (0, 1):
        where = [jax.random.randint(jax.random.fold_in(rng, axis), (), 0, length) for axis, length in enumerate(values.shape)]
        where[longest] = (where[longest] + shift) % values.shape[longest]
        spots.append(tuple(where))
    return values.at[spots[0]].set(smallest).at[spots[1]].set(largest)


def block_levels(stream_key, dims, split, smallest, high):
    gain = 1.0
    for axis_at, shards_of in split:
        steps = jax.random.uniform(jax.random.fold_in(jax.random.fold_in(stream_key, 6), axis_at), (shards_of,), jnp.float32, smallest / len(split), high / len(split))
        gain = gain * jnp.repeat(jnp.exp(steps), dims[axis_at] // shards_of).reshape((-1,) + (1,) * (len(dims) - 1 - axis_at))
    return gain


def bell_draw(stream_key, extent, scale, limit, split=(), kind=jnp.bfloat16):
    loudness = block_levels(stream_key, extent, split, -0.22, 0.18) if split else 1.0
    values = jax.random.normal(stream_key, extent, jnp.float32) * scale * loudness
    return jnp.minimum(jnp.maximum(values, -limit), limit).astype(kind)


def setup_inputs(seed: int = 0) -> dict:
    streams_of = jax.random.split(jax.random.key(seed), 5)
    return {
        "integrals": bell_draw(streams_of[0], (AUX, ROWS, BASIS), 0.12, 0.71875, ((0, 32), (1, 8))),
        "block_mask": set_ends((jax.random.randint(streams_of[1], (AUXB, ROWB, COLB), 0, 5) < 3).astype(jnp.int32), jax.random.fold_in(streams_of[1], 1), 0, 1),
        "coefficients": bell_draw(streams_of[2], (BASIS, OCC), BASIS ** -0.5, 0.0625, ((0, 32),)),
        "occ_index": set_ends(jax.random.randint(streams_of[3], (OCCB,), 0, OCC), jax.random.fold_in(streams_of[3], 1), 0, OCC - 1).astype(jnp.int32),
    }


def half_block(args):
    block, mask_block, batch = args
    rows = jnp.repeat(jnp.repeat(mask_block, ROW_BLK, axis=0), COL_BLK, axis=1).astype(jnp.bfloat16)
    screened = block * rows[None, :, :]
    flat = screened.reshape(P_DEV * ROWS, BASIS)
    return jnp.dot(flat, batch, preferred_element_type=jnp.float32).astype(jnp.bfloat16).reshape(P_DEV, ROWS, OCCB)


def reference(integrals, block_mask, coefficients, occ_index):
    picker = (jnp.arange(OCC, dtype=jnp.int32)[:, None] == occ_index[None, :]).astype(jnp.bfloat16)
    batch = jnp.dot(coefficients, picker, preferred_element_type=jnp.float32).astype(jnp.bfloat16)
    blocks = integrals.reshape(AUXB, P_DEV, ROWS, BASIS)
    half = lax.map(lambda pair: half_block((pair[0], pair[1], batch)), (blocks, block_mask))
    half = half.reshape(AUX, N_ROW, ROW_DEV, OCCB).astype(jnp.float32)
    bands = []
    for j in range(BANDS):
        other = jnp.roll(half, j, axis=1)
        bands.append(jnp.einsum("pgmi,pgni->gmn", half, other))
    result = jnp.stack(bands, axis=2)
    return result.reshape(ROWS, BANDS * ROW_DEV)
```

```python
import jax
import jax.numpy as jnp
from jax import lax
from jax.experimental import pallas as pl
from jax.experimental.pallas import tpu as pltpu
from jax.sharding import Mesh, PartitionSpec as P

BANDS = 3
COL_BLK = 500
HALF = 256
WIN = 2 * HALF
ALIGN = 16
ROW_BLK = 64

AUX = ("zh", "x", "core")
CHIPS = ("zh", "x")
ROW = ("zl", "y")


def window_offset(q):
    return (COL_BLK * q) % ALIGN


def pick_kernel(cols, occ_ref, coef_ref, out_ref):
    rows, occ_all = coef_ref.shape
    batch = occ_ref.shape[1]
    chip = lax.axis_index("zh") * lax.axis_size("x") + lax.axis_index("x")
    start = window_offset(chip) + cols * lax.axis_index("core")
    picker = lax.broadcasted_iota(jnp.int32, (occ_all, batch), 0) == occ_ref[...]
    picked = jnp.dot(
        coef_ref[...],
        picker.astype(jnp.float32).astype(jnp.bfloat16),
        preferred_element_type=jnp.float32,
    ).astype(jnp.bfloat16)
    source = lax.broadcasted_iota(jnp.int32, (rows, HALF), 0)
    place = lax.broadcasted_iota(jnp.int32, (rows, HALF), 1)
    shift = ((source + start) & (HALF - 1)) == place
    window = lax.dot_general(
        picked,
        shift.astype(jnp.float32).astype(jnp.bfloat16),
        (((0,), (0,)), ((), ())),
        preferred_element_type=jnp.float32,
    ).astype(jnp.bfloat16)
    for peer in range(out_ref.shape[0]):
        out_ref[peer] = window


def half_kernel(mask_ref, own_ref, other_ref, integrals_ref, out_ref, blocks, sems):
    chips, batch, _ = own_ref.shape
    p_local, basis, rows = integrals_ref.shape
    core = lax.axis_index("core")
    ends = [COL_BLK * q - window_offset(q) + WIN for q in range(chips)]
    copies = []
    begin = 0
    for q in range(chips):
        span = pl.ds(begin, ends[q] - begin)
        copies.append(
            pltpu.make_async_copy(
                integrals_ref.at[:, span, :], blocks.at[:, span, :], sems.at[q]
            )
        )
        copies[-1].start()
        begin = ends[q]
    lane = lax.broadcasted_iota(jnp.int32, (batch, HALF), 1)
    column = lax.broadcasted_iota(jnp.int32, (1, 2 * rows), 1) % rows
    zero = jnp.zeros((batch, HALF), jnp.bfloat16)
    totals = [jnp.zeros((batch, 2 * rows), jnp.float32) for _ in range(p_local // 2)]
    for q in range(chips):
        own, other = own_ref[q], other_ref[q]
        edge_own = window_offset(q) + (COL_BLK // 2) * core
        edge_other = window_offset(q) + (COL_BLK // 2) * (1 - core)
        low = jnp.where(lane >= edge_own, own, zero) + jnp.where(lane >= edge_other, other, zero)
        high = jnp.where(lane < edge_own, own, zero) + jnp.where(lane < edge_other, other, zero)
        window = jnp.concatenate([low, high], axis=1)
        keep = jnp.where(
            column < ROW_BLK, mask_ref[0, q], mask_ref[1, q]
        ).astype(jnp.float32)
        copies[q].wait()
        span = pl.ds(ends[q] - WIN, WIN)
        for pair in range(p_local // 2):
            block = jnp.concatenate(
                [blocks[2 * pair, span, :], blocks[2 * pair + 1, span, :]], axis=1
            )
            product = jnp.dot(window, block, preferred_element_type=jnp.float32)
            totals[pair] = totals[pair] + product * keep
    for p in range(p_local):
        part = totals[p // 2][:, (p % 2) * rows : (p % 2 + 1) * rows]
        out_ref[p * batch : (p + 1) * batch, :] = part.astype(jnp.bfloat16)


def band_kernel(rows_dev, half_ref, previous_ref, farther_ref, own_ref, send_ref):
    depth, rows = half_ref.shape
    core = lax.axis_index("core")
    out_row = lax.broadcasted_iota(jnp.int32, (rows, rows), 0)
    in_row = lax.broadcasted_iota(jnp.int32, (rows, rows), 1)
    mine = out_row < rows // 2
    local = jnp.where(mine, out_row, out_row - rows // 2)
    parity = jnp.where(mine, core, 1 - core)
    wanted = (local // rows_dev) * (2 * rows_dev) + parity * rows_dev + local % rows_dev
    order = (wanted == in_row).astype(jnp.float32).astype(jnp.bfloat16)
    left = lax.dot_general(
        order, half_ref[...], (((1,), (1,)), ((), ())), preferred_element_type=jnp.float32
    ).astype(jnp.bfloat16)
    for j, ref in enumerate((half_ref, previous_ref, farther_ref)):
        product = jnp.dot(left, ref[...], preferred_element_type=jnp.float32)
        own_ref[:, j * rows : (j + 1) * rows] = product[: rows // 2]
        send_ref[:, j * rows : (j + 1) * rows] = product[rows // 2 :]


def from_behind(block, axis, distance):
    devices = range(lax.axis_size(axis))
    route = [((i - distance) % len(devices), i) for i in devices]
    return lax.ppermute(block, axis, route)


def per_device(integrals, block_mask, coefficients, occ_index):
    p_local, r_local, basis = integrals.shape
    cols, _ = coefficients.shape
    batch = occ_index.shape[0]
    chips = lax.axis_size(CHIPS)
    cores = lax.axis_size("core")
    whole = pl.BlockSpec(memory_space=pltpu.VMEM)
    scalars = pl.BlockSpec(memory_space=pltpu.SMEM)

    windows = pl.pallas_call(
        lambda *refs: pick_kernel(cols, *refs),
        out_shape=jax.ShapeDtypeStruct((chips, batch, HALF), jnp.bfloat16),
        in_specs=[whole, whole],
        out_specs=whole,
        name="pick",
    )(occ_index.reshape(1, batch), coefficients)
    own = lax.all_to_all(windows, CHIPS, 0, 0)
    other = lax.ppermute(own, "core", [(0, 1), (1, 0)])

    half = pl.pallas_call(
        half_kernel,
        out_shape=jax.ShapeDtypeStruct((p_local * batch, r_local), jnp.bfloat16),
        in_specs=[scalars, whole, whole, pl.BlockSpec(memory_space=pl.ANY)],
        out_specs=whole,
        scratch_shapes=[
            pltpu.VMEM((p_local, basis, r_local), jnp.bfloat16),
            pltpu.SemaphoreType.DMA((chips,)),
        ],
        compiler_params=pltpu.CompilerParams(vmem_limit_bytes=24 * 1024 * 1024),
        name="half",
    )(block_mask[0], own, other, jnp.swapaxes(integrals, 1, 2))

    previous = from_behind(half, ROW, 1)
    farther = from_behind(half, ROW, 2)
    rows_dev = r_local // (chips * cores)
    part = jax.ShapeDtypeStruct((r_local // cores, BANDS * r_local), jnp.float32)
    kept, sent = pl.pallas_call(
        lambda *refs: band_kernel(rows_dev, *refs),
        out_shape=(part, part),
        in_specs=[whole] * 3,
        out_specs=(whole, whole),
        name="bands",
    )(half, previous, farther)
    chip_sum = kept + lax.ppermute(sent, "core", [(0, 1), (1, 0)])
    pieces = lax.all_to_all(
        chip_sum.reshape(chips, rows_dev, BANDS * r_local), CHIPS, 0, 0
    )
    return jnp.sum(pieces, axis=0)


def solution(mesh):
    fine = Mesh(mesh.devices.reshape(4, 4, 2, 2, 4), AUX + ROW)
    in_specs = (P(AUX, ROW, None), P(AUX, ROW, None), P(AUX, None), P())
    out_specs = P(ROW + AUX, None)
    return jax.shard_map(
        per_device, mesh=fine, in_specs=in_specs, out_specs=out_specs, check_vma=False
    )
```

```python
import jax
import jax.numpy as jnp
from jax import lax
from jax.experimental import pallas as pl
from jax.experimental.pallas import tpu as pltpu
from jax.sharding import Mesh, PartitionSpec as P

BANDS = 3
COL_BLK = 500
HALF = 256
WIN = 2 * HALF
ALIGN = 16
ROW_BLK = 64
MIB = 1024 * 1024

ZH, X, CORE, ZL, Y = "zh", "x", "core", "zl", "y"
AUX = (ZH, X, CORE)
ROW = (ZL, Y)


WHOLE = pl.BlockSpec(memory_space=pltpu.VMEM)
ANYWHERE = pl.BlockSpec(memory_space=pl.ANY)


def window_offset(q):
    return (COL_BLK * q) % ALIGN


def pick_kernel(occ_hbm, coef_hbm, mask_hbm, window_ref, keep_ref, occ_ref, coef_ref, mask_ref, sems):
    copies = [
        pltpu.make_async_copy(occ_hbm, occ_ref, sems.at[0]),
        pltpu.make_async_copy(coef_hbm, coef_ref, sems.at[1]),
        pltpu.make_async_copy(mask_hbm, mask_ref, sems.at[2]),
    ]
    for copy in copies:
        copy.start()
    cols, occ_all = coef_ref.shape
    batch = occ_ref.shape[1]
    chip = lax.axis_index(ZH) * lax.axis_size(X) + lax.axis_index(X)
    start = window_offset(chip) + cols * lax.axis_index(CORE)
    source = lax.broadcasted_iota(jnp.int32, (cols, HALF), 0)
    place = lax.broadcasted_iota(jnp.int32, (cols, HALF), 1)
    shift = ((source + start) & (HALF - 1)) == place
    copies[0].wait()
    picker = lax.broadcasted_iota(jnp.int32, (occ_all, batch), 0) == occ_ref[...]
    copies[2].wait()
    lane = lax.broadcasted_iota(jnp.int32, (1, keep_ref.shape[1]), 1)
    for q in range(keep_ref.shape[0]):
        keep = jnp.where(lane < ROW_BLK, mask_ref[0, q], mask_ref[1, q])
        keep_ref[q : q + 1, :] = keep.astype(jnp.float32)
    copies[1].wait()
    picked = jnp.dot(
        coef_ref[...],
        picker.astype(jnp.float32).astype(jnp.bfloat16),
        preferred_element_type=jnp.float32,
    ).astype(jnp.bfloat16)
    window_ref[0] = lax.dot_general(
        picked,
        shift.astype(jnp.float32).astype(jnp.bfloat16),
        (((0,), (0,)), ((), ())),
        preferred_element_type=jnp.float32,
    ).astype(jnp.bfloat16)


def stage_kernel(integrals_ref, total_ref):
    del integrals_ref
    total_ref[...] = jnp.zeros_like(total_ref)


def half_kernel(distance, last, keep_ref, own_ref, other_ref, integrals_ref, before_ref, out_ref):
    slots, batch, _ = own_ref.shape
    p_local, _, rows = integrals_ref.shape
    zh, zl, core = lax.axis_index(ZH), lax.axis_index(ZL), lax.axis_index(CORE)
    layers, width = lax.axis_size(ZH), lax.axis_size(X)
    x = lax.rem(lax.axis_index(X) + distance, width)
    near = jnp.where(zl == 0, layers - 1, 1)
    lane = lax.broadcasted_iota(jnp.int32, (batch, HALF), 1)
    zero = jnp.zeros((batch, HALF), jnp.bfloat16)
    pairs = p_local // 2
    totals = [before_ref[pair] for pair in range(pairs)]
    for slot, shift in enumerate((0, near, layers - near, 2)):
        q = lax.rem(zh + shift, layers) * width + x
        offset = lax.rem(COL_BLK * q, ALIGN)
        own, other = own_ref[slot], other_ref[slot]
        edge_own = offset + (COL_BLK // 2) * core
        edge_other = offset + (COL_BLK // 2) * (1 - core)
        low = jnp.where(lane >= edge_own, own, zero) + jnp.where(lane >= edge_other, other, zero)
        high = jnp.where(lane < edge_own, own, zero) + jnp.where(lane < edge_other, other, zero)
        window = jnp.concatenate([low, high], axis=1)
        keep = keep_ref[pl.ds(q, 1), :]
        keep = jnp.concatenate([keep, keep], axis=1)
        span = pl.ds(pl.multiple_of(COL_BLK * q - offset, ALIGN), WIN)
        for pair in range(pairs):
            block = jnp.concatenate(
                [integrals_ref[2 * pair, span, :], integrals_ref[2 * pair + 1, span, :]], axis=1
            )
            product = jnp.dot(window, block, preferred_element_type=jnp.float32)
            totals[pair] = totals[pair] + product * keep
    if last:
        for p in range(p_local):
            part = totals[p // 2][:, (p % 2) * rows : (p % 2 + 1) * rows]
            out_ref[p * batch : (p + 1) * batch, :] = part.astype(jnp.bfloat16)
    else:
        for pair in range(pairs):
            out_ref[pair] = totals[pair]


def band_kernel(rows_dev, half_ref, previous_ref, farther_ref, own_ref, send_ref):
    rows = half_ref.shape[1]
    core = lax.axis_index(CORE)
    out_row = lax.broadcasted_iota(jnp.int32, (rows, rows), 0)
    in_row = lax.broadcasted_iota(jnp.int32, (rows, rows), 1)
    mine = out_row < rows // 2
    local = jnp.where(mine, out_row, out_row - rows // 2)
    parity = jnp.where(mine, core, 1 - core)
    wanted = (local // rows_dev) * (2 * rows_dev) + parity * rows_dev + local % rows_dev
    order = (wanted == in_row).astype(jnp.float32).astype(jnp.bfloat16)
    left = lax.dot_general(
        order, half_ref[...], (((1,), (1,)), ((), ())), preferred_element_type=jnp.float32
    ).astype(jnp.bfloat16)
    for j, ref in enumerate((half_ref, previous_ref, farther_ref)):
        product = jnp.dot(left, ref[...], preferred_element_type=jnp.float32)
        own_ref[:, j * rows : (j + 1) * rows] = product[: rows // 2]
        send_ref[:, j * rows : (j + 1) * rows] = product[rows // 2 :]


def from_behind(block, axis, distance):
    devices = range(lax.axis_size(axis))
    route = [((i - distance) % len(devices), i) for i in devices]
    return lax.ppermute(block, axis, route)


def along_z(block, even, odd):
    height = lax.axis_size((ZH, ZL))
    route = [((z + (odd if z % 2 else even)) % height, z) for z in range(height)]
    return lax.ppermute(block, (ZH, ZL), route)


def other_core(block):
    return lax.ppermute(block, CORE, [(0, 1), (1, 0)])


def params(mib):
    return pltpu.CompilerParams(vmem_limit_bytes=mib * MIB)


def per_device(integrals, block_mask, coefficients, occ_index):
    p_local, r_local, basis = integrals.shape
    cols, occ_all = coefficients.shape
    batch = occ_index.shape[0]
    chips = lax.axis_size((ZH, X))
    mask = block_mask[0]

    window, keep = pl.pallas_call(
        pick_kernel,
        out_shape=(
            jax.ShapeDtypeStruct((1, batch, HALF), jnp.bfloat16),
            jax.ShapeDtypeStruct((chips, r_local), jnp.float32),
        ),
        in_specs=[ANYWHERE] * 3,
        out_specs=(WHOLE, WHOLE),
        scratch_shapes=[
            pltpu.VMEM((1, batch), jnp.int32),
            pltpu.VMEM((cols, occ_all), jnp.bfloat16),
            pltpu.SMEM(mask.shape, jnp.int32),
            pltpu.SemaphoreType.DMA((3,)),
        ],
        name="pick",
    )(occ_index.reshape(1, batch), coefficients, mask)

    by_column, window = lax.optimization_barrier((jnp.swapaxes(integrals, 1, 2), window))
    layers = [window, along_z(window, -1, 1), along_z(window, 2, -2), along_z(window, -3, 3)]
    running = jax.ShapeDtypeStruct((p_local // 2, batch, 2 * r_local), jnp.float32)
    total = pl.pallas_call(
        stage_kernel,
        out_shape=running,
        in_specs=[WHOLE],
        out_specs=WHOLE,
        compiler_params=params(12),
        name="stage",
    )(by_column)
    layers, by_column, total = lax.optimization_barrier((layers, by_column, total))
    stack = jnp.concatenate(layers, axis=0)

    for distance in (0, 1, 3, 2):
        own = stack if distance == 0 else from_behind(stack, X, -distance)
        last = distance == 2
        out = jax.ShapeDtypeStruct((p_local * batch, r_local), jnp.bfloat16) if last else running
        total = pl.pallas_call(
            lambda *refs, distance=distance, last=last: half_kernel(distance, last, *refs),
            out_shape=out,
            in_specs=[WHOLE] * 5,
            out_specs=WHOLE,
            compiler_params=params(12),
            cost_estimate=pl.CostEstimate(
                flops=2 * batch * WIN * 4 * p_local * r_local,
                bytes_accessed=by_column.size // 2,
                transcendentals=0,
            ),
            name="half",
        )(keep, own, other_core(own), by_column, total)
    half = total

    previous = from_behind(half, ROW, 1)
    farther = from_behind(half, ROW, 2)
    rows_dev = r_local // (chips * lax.axis_size(CORE))
    part = jax.ShapeDtypeStruct((chips * rows_dev, BANDS * r_local), jnp.float32)
    kept, sent = pl.pallas_call(
        lambda *refs: band_kernel(rows_dev, *refs),
        out_shape=(part, part),
        in_specs=[WHOLE] * 3,
        out_specs=(WHOLE, WHOLE),
        compiler_params=params(4),
        name="bands",
    )(half, previous, farther)
    chip_sum = kept + other_core(sent)
    pieces = lax.all_to_all(
        chip_sum.reshape(chips, rows_dev, BANDS * r_local), (ZH, X), 0, 0
    )
    return jnp.sum(pieces, axis=0)


def solution(mesh):
    fine = Mesh(mesh.devices.reshape(4, 4, 2, 2, 4), AUX + ROW)
    in_specs = (P(AUX, ROW, None), P(AUX, ROW, None), P(AUX, None), P())
    out_specs = P(ROW + AUX, None)
    return jax.shard_map(
        per_device, mesh=fine, in_specs=in_specs, out_specs=out_specs, check_vma=False
    )
```

```python
import jax
import jax.numpy as jnp
from jax import lax
from jax.experimental import pallas as pl
from jax.experimental.pallas import tpu as pltpu
from jax.sharding import Mesh, PartitionSpec as P

BANDS = 3
COL_BLK = 500
WIN = 512
ALIGN = 16
ROW_BLK = 64
MIB = 1024 * 1024

ZH, X, CORE, ZL, Y = "zh", "x", "core", "zl", "y"
AUX = (ZH, X, CORE)
ROW = (ZL, Y)


WHOLE = pl.BlockSpec(memory_space=pltpu.VMEM)


def window_offset(q):
    return (COL_BLK * q) % ALIGN


def pick_kernel(cols, small_ref, own_ref, other_ref, window_ref):
    batch = small_ref.shape[1]
    chip = lax.axis_index(ZH) * lax.axis_size(X) + lax.axis_index(X)
    core = lax.axis_index(CORE)
    offset = window_offset(chip)
    picker = lax.broadcasted_iota(jnp.int32, (own_ref.shape[1], batch), 0) == small_ref[0:1, :]
    picker = picker.astype(jnp.float32).astype(jnp.bfloat16)
    window = jnp.zeros((batch, WIN), jnp.float32)
    for ref, start in ((own_ref, offset + cols * core), (other_ref, offset + cols * (1 - core))):
        picked = jnp.dot(ref[...], picker, preferred_element_type=jnp.float32)
        source = lax.broadcasted_iota(jnp.int32, (ref.shape[0], WIN), 0)
        place = lax.broadcasted_iota(jnp.int32, (ref.shape[0], WIN), 1)
        shift = (source + start == place).astype(jnp.float32).astype(jnp.bfloat16)
        window = window + lax.dot_general(
            picked.astype(jnp.bfloat16),
            shift,
            (((0,), (0,)), ((), ())),
            preferred_element_type=jnp.float32,
        )
    window_ref[...] = window.astype(jnp.bfloat16)


def stack_kernel(window_ref, first_ref, second_ref, out_ref):
    core = lax.axis_index(CORE)

    @pl.when(core == 0)
    def _():
        out_ref[0] = window_ref[...]

    @pl.when(core != 0)
    def _():
        out_ref[0] = second_ref[...]

    out_ref[1] = first_ref[...]


def stage_kernel(integrals_ref, total_ref):
    del integrals_ref
    total_ref[...] = jnp.zeros_like(total_ref)


def half_kernel(distance, last, small_ref, own_ref, other_ref, integrals_ref, before_ref, out_ref):
    slots, batch, _ = own_ref.shape
    p_local, _, rows = integrals_ref.shape
    zh, zl, core = lax.axis_index(ZH), lax.axis_index(ZL), lax.axis_index(CORE)
    layers, width = lax.axis_size(ZH), lax.axis_size(X)
    x = lax.axis_index(X) ^ distance
    near = jnp.where(zl == 0, layers - 1, 1)
    pairs = p_local // 2
    totals = [before_ref[pair] for pair in range(pairs)]
    masks = small_ref[...].astype(jnp.float32)
    entry = lax.broadcasted_iota(jnp.int32, masks.shape, 1)
    column = lax.broadcasted_iota(jnp.int32, (1, 2 * rows), 1) % rows
    for ref, holder in ((own_ref, core), (other_ref, 1 - core)):
        for slot in range(slots):
            even = 0 if slot == 0 else 2
            odd = layers - near if slot == 0 else near
            q = lax.rem(zh + jnp.where(holder == 0, even, odd), layers) * width + x
            offset = lax.rem(COL_BLK * q, ALIGN)
            chosen = jnp.sum(jnp.where(entry == q, masks, 0.0), axis=1, keepdims=True)
            keep = jnp.where(column < ROW_BLK, chosen[1:2, :], chosen[2:3, :])
            span = pl.ds(pl.multiple_of(COL_BLK * q - offset, ALIGN), WIN)
            for pair in range(pairs):
                block = jnp.concatenate(
                    [integrals_ref[2 * pair, span, :], integrals_ref[2 * pair + 1, span, :]],
                    axis=1,
                )
                product = jnp.dot(ref[slot], block, preferred_element_type=jnp.float32)
                totals[pair] = totals[pair] + product * keep
    if last:
        for p in range(p_local):
            part = totals[p // 2][:, (p % 2) * rows : (p % 2 + 1) * rows]
            out_ref[p * batch : (p + 1) * batch, :] = part.astype(jnp.bfloat16)
    else:
        for pair in range(pairs):
            out_ref[pair] = totals[pair]


def near_kernel(rows_dev, half_ref, previous_ref, left_ref, near_ref):
    rows = half_ref.shape[1]
    core = lax.axis_index(CORE)
    out_row = lax.broadcasted_iota(jnp.int32, (rows, rows), 0)
    in_row = lax.broadcasted_iota(jnp.int32, (rows, rows), 1)
    mine = out_row < rows // 2
    local = jnp.where(mine, out_row, out_row - rows // 2)
    parity = jnp.where(mine, core, 1 - core)
    wanted = (local // rows_dev) * (2 * rows_dev) + parity * rows_dev + local % rows_dev
    order = (wanted == in_row).astype(jnp.float32).astype(jnp.bfloat16)
    left = lax.dot_general(
        order, half_ref[...], (((1,), (1,)), ((), ())), preferred_element_type=jnp.float32
    ).astype(jnp.bfloat16)
    left_ref[...] = left
    for j, ref in enumerate((half_ref, previous_ref)):
        near_ref[:, j * rows : (j + 1) * rows] = jnp.dot(
            left, ref[...], preferred_element_type=jnp.float32
        )


def band_kernel(left_ref, near_ref, farther_ref, own_ref, send_ref):
    rows = left_ref.shape[0]
    done = near_ref.shape[1]
    own_ref[:, :done] = near_ref[: rows // 2, :]
    send_ref[:, :done] = near_ref[rows // 2 :, :]
    product = jnp.dot(left_ref[...], farther_ref[...], preferred_element_type=jnp.float32)
    own_ref[:, done:] = product[: rows // 2]
    send_ref[:, done:] = product[rows // 2 :]


def from_behind(block, axis, distance):
    devices = range(lax.axis_size(axis))
    route = [((i - distance) % len(devices), i) for i in devices]
    return lax.ppermute(block, axis, route)


def along_z(block, steps):
    height, halves, cores = (lax.axis_size(a) for a in ((ZH, ZL), ZL, CORE))

    def place(z, core):
        return (z // halves * cores + core) * halves + z % halves

    route = [
        (place((z + steps[core, z % halves]) % height, core), place(z, core))
        for z in range(height)
        for core in range(cores)
        if (core, z % halves) in steps
    ]
    return lax.ppermute(block, (ZH, CORE, ZL), route)


def across_x(block, distance):
    return lax.ppermute(block, X, [(i ^ distance, i) for i in range(lax.axis_size(X))])


def other_core(block):
    return lax.ppermute(block, CORE, [(0, 1), (1, 0)])


def params(mib):
    return pltpu.CompilerParams(vmem_limit_bytes=mib * MIB)


def per_device(integrals, block_mask, coefficients, occ_index):
    p_local, r_local, basis = integrals.shape
    cols = coefficients.shape[0]
    batch = occ_index.shape[0]
    chips = lax.axis_size((ZH, X))
    mask = block_mask[0]

    other_coefficients = other_core(coefficients)
    small = jnp.concatenate(
        [occ_index[None, :], jnp.pad(mask, ((0, 0), (0, batch - mask.shape[1])))], axis=0
    )
    padded = jnp.pad(coefficients, ((0, -cols % ALIGN), (0, 0)))
    window = pl.pallas_call(
        lambda *refs: pick_kernel(cols, *refs),
        out_shape=jax.ShapeDtypeStruct((batch, WIN), jnp.bfloat16),
        in_specs=[WHOLE] * 3,
        out_specs=WHOLE,
        compiler_params=params(4),
        name="pick",
    )(small, padded, other_coefficients)

    by_column, window = lax.optimization_barrier((jnp.swapaxes(integrals, 1, 2), window))
    second = along_z(window, {(1, 0): 2, (1, 1): -2})
    first = along_z(window, {(0, 0): -3, (0, 1): 3, (1, 0): -1, (1, 1): 1})
    running = jax.ShapeDtypeStruct((p_local // 2, batch, 2 * r_local), jnp.float32)
    total = pl.pallas_call(
        stage_kernel,
        out_shape=running,
        in_specs=[WHOLE],
        out_specs=WHOLE,
        compiler_params=params(12),
        name="stage",
    )(by_column)
    first, by_column, total = lax.optimization_barrier((first, by_column, total))
    stack = pl.pallas_call(
        stack_kernel,
        out_shape=jax.ShapeDtypeStruct((2, batch, WIN), jnp.bfloat16),
        in_specs=[WHOLE] * 3,
        out_specs=WHOLE,
        compiler_params=params(4),
        name="stack",
    )(window, first, second)

    for distance in (0, 2, 1, 3):
        own = stack if distance == 0 else across_x(stack, distance)
        if distance == 2:
            own, total = lax.optimization_barrier((own, total))
        last = distance == 3
        out = jax.ShapeDtypeStruct((p_local * batch, r_local), jnp.bfloat16) if last else running
        total = pl.pallas_call(
            lambda *refs, distance=distance, last=last: half_kernel(distance, last, *refs),
            out_shape=out,
            in_specs=[WHOLE] * 5,
            out_specs=WHOLE,
            compiler_params=params(12),
            cost_estimate=pl.CostEstimate(flops=1, bytes_accessed=4096, transcendentals=0)
            if distance == 0
            else pl.CostEstimate(
                flops=2 * batch * WIN * 4 * p_local * r_local,
                bytes_accessed=by_column.size // 2,
                transcendentals=0,
            ),
            name="half",
        )(small, own, other_core(own), by_column, total)
    half = total

    previous = from_behind(half, ROW, 1)
    farther = from_behind(half, ROW, 2)
    rows_dev = r_local // (chips * lax.axis_size(CORE))
    left, near = pl.pallas_call(
        lambda *refs: near_kernel(rows_dev, *refs),
        out_shape=(
            jax.ShapeDtypeStruct(half.shape[::-1], jnp.bfloat16),
            jax.ShapeDtypeStruct((r_local, (BANDS - 1) * r_local), jnp.float32),
        ),
        in_specs=[WHOLE] * 2,
        out_specs=(WHOLE, WHOLE),
        compiler_params=params(4),
        cost_estimate=pl.CostEstimate(flops=1, bytes_accessed=4096, transcendentals=0),
        name="near",
    )(half, previous)
    part = jax.ShapeDtypeStruct((chips * rows_dev, BANDS * r_local), jnp.float32)
    kept, sent = pl.pallas_call(
        band_kernel,
        out_shape=(part, part),
        in_specs=[WHOLE] * 3,
        out_specs=(WHOLE, WHOLE),
        compiler_params=params(4),
        name="bands",
    )(left, near, farther)
    chip_sum = kept + other_core(sent)
    pieces = lax.all_to_all(
        chip_sum.reshape(chips, rows_dev, BANDS * r_local), (ZH, X), 0, 0
    )
    return jnp.sum(pieces, axis=0)


def solution(mesh):
    fine = Mesh(mesh.devices.reshape(4, 4, 2, 2, 4), AUX + ROW)
    in_specs = (P(AUX, ROW, None), P(AUX, ROW, None), P(AUX, None), P())
    out_specs = P(ROW + AUX, None)
    return jax.shard_map(
        per_device, mesh=fine, in_specs=in_specs, out_specs=out_specs, check_vma=False
    )
```

```python
import jax
import jax.numpy as jnp
from jax import lax
from jax.experimental import pallas as pl
from jax.experimental.pallas import tpu as pltpu
from jax.sharding import Mesh, PartitionSpec as P

BANDS = 3
COL_BLK = 500
WIN = 512
ALIGN = 16
ROW_BLK = 64
MIB = 1024 * 1024

ZH, X, CORE, ZL, Y = "zh", "x", "core", "zl", "y"
AUX = (ZH, X, CORE)
ROW = (ZL, Y)


WHOLE = pl.BlockSpec(memory_space=pltpu.VMEM)


def window_offset(q):
    return (COL_BLK * q) % ALIGN


def pick_kernel(cols, small_ref, own_ref, other_ref, window_ref):
    batch = small_ref.shape[1]
    chip = lax.axis_index(ZH) * lax.axis_size(X) + lax.axis_index(X)
    core = lax.axis_index(CORE)
    offset = window_offset(chip)
    picker = lax.broadcasted_iota(jnp.int32, (own_ref.shape[1], batch), 0) == small_ref[0:1, :]
    picker = picker.astype(jnp.float32).astype(jnp.bfloat16)
    window = jnp.zeros((batch, WIN), jnp.float32)
    for ref, start in ((own_ref, offset + cols * core), (other_ref, offset + cols * (1 - core))):
        picked = jnp.dot(ref[...], picker, preferred_element_type=jnp.float32)
        source = lax.broadcasted_iota(jnp.int32, (ref.shape[0], WIN), 0)
        place = lax.broadcasted_iota(jnp.int32, (ref.shape[0], WIN), 1)
        shift = (source + start == place).astype(jnp.float32).astype(jnp.bfloat16)
        window = window + lax.dot_general(
            picked.astype(jnp.bfloat16),
            shift,
            (((0,), (0,)), ((), ())),
            preferred_element_type=jnp.float32,
        )
    window_ref[...] = window.astype(jnp.bfloat16)


def stack_kernel(window_ref, first_ref, second_ref, out_ref):
    core = lax.axis_index(CORE)

    @pl.when(core == 0)
    def _():
        out_ref[0] = window_ref[...]

    @pl.when(core != 0)
    def _():
        out_ref[0] = second_ref[...]

    out_ref[1] = first_ref[...]


def stage_kernel(integrals_ref, total_ref):
    del integrals_ref
    total_ref[...] = jnp.zeros_like(total_ref)


def half_kernel(parts, last, small_ref, integrals_ref, before_ref, *refs):
    *stack_refs, out_ref = refs
    slots, batch, _ = stack_refs[0].shape
    p_local, _, rows = integrals_ref.shape
    zh, zl, core = lax.axis_index(ZH), lax.axis_index(ZL), lax.axis_index(CORE)
    layers, width = lax.axis_size(ZH), lax.axis_size(X)
    near = jnp.where(zl == 0, layers - 1, 1)
    pairs = p_local // 2
    totals = [before_ref[pair] for pair in range(pairs)]
    masks = small_ref[...].astype(jnp.float32)
    entry = lax.broadcasted_iota(jnp.int32, masks.shape, 1)
    column = lax.broadcasted_iota(jnp.int32, (1, 2 * rows), 1) % rows
    for ref, (distance, mine) in zip(stack_refs, parts):
        x = lax.rem(lax.axis_index(X) + distance, width)
        holder = core if mine else 1 - core
        for slot in range(slots):
            even = 0 if slot == 0 else 2
            odd = layers - near if slot == 0 else near
            q = lax.rem(zh + jnp.where(holder == 0, even, odd), layers) * width + x
            offset = lax.rem(COL_BLK * q, ALIGN)
            chosen = jnp.sum(jnp.where(entry == q, masks, 0.0), axis=1, keepdims=True)
            keep = jnp.where(column < ROW_BLK, chosen[1:2, :], chosen[2:3, :])
            span = pl.ds(pl.multiple_of(COL_BLK * q - offset, ALIGN), WIN)
            for pair in range(pairs):
                block = jnp.concatenate(
                    [integrals_ref[2 * pair, span, :], integrals_ref[2 * pair + 1, span, :]],
                    axis=1,
                )
                product = jnp.dot(ref[slot], block, preferred_element_type=jnp.float32)
                totals[pair] = totals[pair] + product * keep
    if last:
        for p in range(p_local):
            part = totals[p // 2][:, (p % 2) * rows : (p % 2 + 1) * rows]
            out_ref[p * batch : (p + 1) * batch, :] = part.astype(jnp.bfloat16)
    else:
        for pair in range(pairs):
            out_ref[pair] = totals[pair]


def turned(index, size):
    return (index + size // 2) % size


def near_kernel(rows_dev, half_ref, previous_ref, left_ref, near_ref):
    rows = half_ref.shape[1]
    core = lax.axis_index(CORE)
    out_row = lax.broadcasted_iota(jnp.int32, (rows, rows), 0)
    in_row = lax.broadcasted_iota(jnp.int32, (rows, rows), 1)
    mine = out_row < rows // 2
    local = jnp.where(mine, out_row, out_row - rows // 2)
    parity = jnp.where(mine, core, 1 - core)
    place = local // rows_dev
    width = lax.axis_size(X)
    chip = turned(place // width, lax.axis_size(ZH)) * width + turned(place % width, width)
    wanted = chip * (2 * rows_dev) + parity * rows_dev + local % rows_dev
    order = (wanted == in_row).astype(jnp.float32).astype(jnp.bfloat16)
    left = lax.dot_general(
        order, half_ref[...], (((1,), (1,)), ((), ())), preferred_element_type=jnp.float32
    ).astype(jnp.bfloat16)
    left_ref[...] = left
    for j, ref in enumerate((half_ref, previous_ref)):
        near_ref[:, j * rows : (j + 1) * rows] = jnp.dot(
            left, ref[...], preferred_element_type=jnp.float32
        )


def band_kernel(left_ref, near_ref, farther_ref, own_ref, send_ref):
    rows = left_ref.shape[0]
    done = near_ref.shape[1]
    own_ref[:, :done] = near_ref[: rows // 2, :]
    send_ref[:, :done] = near_ref[rows // 2 :, :]
    product = jnp.dot(left_ref[...], farther_ref[...], preferred_element_type=jnp.float32)
    own_ref[:, done:] = product[: rows // 2]
    send_ref[:, done:] = product[rows // 2 :]


def from_behind(block, axis, distance):
    devices = range(lax.axis_size(axis))
    route = [((i - distance) % len(devices), i) for i in devices]
    return lax.ppermute(block, axis, route)


def along_z(block, steps):
    height, halves, cores = (lax.axis_size(a) for a in ((ZH, ZL), ZL, CORE))

    def place(z, core):
        return (z // halves * cores + core) * halves + z % halves

    route = [
        (place((z + steps[core, z % halves]) % height, core), place(z, core))
        for z in range(height)
        for core in range(cores)
        if (core, z % halves) in steps
    ]
    return lax.ppermute(block, (ZH, CORE, ZL), route)


def other_core(block):
    return lax.ppermute(block, CORE, [(0, 1), (1, 0)])


def params(mib):
    return pltpu.CompilerParams(vmem_limit_bytes=mib * MIB)


def per_device(integrals, block_mask, coefficients, occ_index):
    p_local, r_local, basis = integrals.shape
    cols = coefficients.shape[0]
    batch = occ_index.shape[0]
    chips = lax.axis_size((ZH, X))
    mask = block_mask[0]

    other_coefficients = other_core(coefficients)
    small = jnp.concatenate(
        [occ_index[None, :], jnp.pad(mask, ((0, 0), (0, batch - mask.shape[1])))], axis=0
    )
    padded = jnp.pad(coefficients, ((0, -cols % ALIGN), (0, 0)))
    window = pl.pallas_call(
        lambda *refs: pick_kernel(cols, *refs),
        out_shape=jax.ShapeDtypeStruct((batch, WIN), jnp.bfloat16),
        in_specs=[WHOLE] * 3,
        out_specs=WHOLE,
        compiler_params=params(4),
        name="pick",
    )(small, padded, other_coefficients)

    by_column, window = lax.optimization_barrier((jnp.swapaxes(integrals, 1, 2), window))
    second = along_z(window, {(1, 0): 2, (1, 1): -2})
    first = along_z(window, {(0, 0): -3, (0, 1): 3, (1, 0): -1, (1, 1): 1})
    running = jax.ShapeDtypeStruct((p_local // 2, batch, 2 * r_local), jnp.float32)
    total = pl.pallas_call(
        stage_kernel,
        out_shape=running,
        in_specs=[WHOLE],
        out_specs=WHOLE,
        compiler_params=params(12),
        name="stage",
    )(by_column)
    first, by_column, total = lax.optimization_barrier((first, by_column, total))
    stack = pl.pallas_call(
        stack_kernel,
        out_shape=jax.ShapeDtypeStruct((2, batch, WIN), jnp.bfloat16),
        in_specs=[WHOLE] * 3,
        out_specs=WHOLE,
        compiler_params=params(4),
        name="stack",
    )(window, first, second)

    def add_products(total, parts, stacks, last=False, cost=None):
        out = jax.ShapeDtypeStruct((p_local * batch, r_local), jnp.bfloat16) if last else running
        return pl.pallas_call(
            lambda *refs: half_kernel(parts, last, *refs),
            out_shape=out,
            in_specs=[WHOLE] * (3 + len(stacks)),
            out_specs=WHOLE,
            compiler_params=params(12),
            cost_estimate=cost
            or pl.CostEstimate(
                flops=2 * batch * WIN * 2 * len(stacks) * p_local * r_local,
                bytes_accessed=by_column.size * len(stacks) // 4,
                transcendentals=0,
            ),
            name="half",
        )(small, by_column, total, *stacks)

    brief = pl.CostEstimate(flops=1, bytes_accessed=4096, transcendentals=0)
    total = add_products(total, [(0, True)], [stack], cost=brief)
    parts, stacks = [(0, False)], [other_core(stack)]
    for distance in (2, 1, 3):
        own = from_behind(stack, X, -distance)
        if distance == 2:
            own, total = lax.optimization_barrier((own, total))
        parts += [(distance, True), (distance, False)]
        stacks += [own, other_core(own)]
        total = add_products(total, parts, stacks, last=distance == 3)
        parts, stacks = [], []
    half = total

    previous = from_behind(half, ROW, 1)
    farther = from_behind(half, ROW, 2)
    rows_dev = r_local // (chips * lax.axis_size(CORE))
    left, near = pl.pallas_call(
        lambda *refs: near_kernel(rows_dev, *refs),
        out_shape=(
            jax.ShapeDtypeStruct(half.shape[::-1], jnp.bfloat16),
            jax.ShapeDtypeStruct((r_local, (BANDS - 1) * r_local), jnp.float32),
        ),
        in_specs=[WHOLE] * 2,
        out_specs=(WHOLE, WHOLE),
        compiler_params=params(4),
        cost_estimate=pl.CostEstimate(flops=1, bytes_accessed=4096, transcendentals=0),
        name="near",
    )(half, previous)
    part = jax.ShapeDtypeStruct((chips * rows_dev, BANDS * r_local), jnp.float32)
    kept, sent = pl.pallas_call(
        band_kernel,
        out_shape=(part, part),
        in_specs=[WHOLE] * 3,
        out_specs=(WHOLE, WHOLE),
        compiler_params=params(4),
        name="bands",
    )(left, near, farther)
    chip_sum = kept + other_core(sent)
    layers, width = lax.axis_size(ZH), lax.axis_size(X)
    order = [
        turned(zh, layers) * width + turned(x, width) for zh in range(layers) for x in range(width)
    ]
    pieces = lax.all_to_all(
        chip_sum.reshape(chips, rows_dev, BANDS * r_local),
        (ZH, X),
        0,
        0,
        axis_index_groups=[order],
    )
    return jnp.sum(pieces, axis=0)


def solution(mesh):
    fine = Mesh(mesh.devices.reshape(4, 4, 2, 2, 4), AUX + ROW)
    in_specs = (P(AUX, ROW, None), P(AUX, ROW, None), P(AUX, None), P())
    out_specs = P(ROW + AUX, None)
    return jax.shard_map(
        per_device, mesh=fine, in_specs=in_specs, out_specs=out_specs, check_vma=False
    )
```

```python
import jax
import jax.numpy as jnp
from jax import lax
from jax.experimental import pallas as pl
from jax.experimental.pallas import tpu as pltpu
from jax.sharding import Mesh, PartitionSpec as P

BANDS = 3
COL_BLK = 500
WIN = 512
ALIGN = 16
ROW_BLK = 64
MIB = 1024 * 1024

ZH, X, CORE, ZL, Y = "zh", "x", "core", "zl", "y"
AUX = (ZH, X, CORE)
ROW = (ZL, Y)


WHOLE = pl.BlockSpec(memory_space=pltpu.VMEM)


def window_offset(q):
    return (COL_BLK * q) % ALIGN


def pick_kernel(cols, small_ref, own_ref, other_ref, window_ref):
    batch = small_ref.shape[1]
    chip = lax.axis_index(ZH) * lax.axis_size(X) + lax.axis_index(X)
    core = lax.axis_index(CORE)
    offset = window_offset(chip)
    picker = lax.broadcasted_iota(jnp.int32, (own_ref.shape[1], batch), 0) == small_ref[0:1, :]
    picker = picker.astype(jnp.float32).astype(jnp.bfloat16)
    window = jnp.zeros((batch, WIN), jnp.float32)
    for ref, start in ((own_ref, offset + cols * core), (other_ref, offset + cols * (1 - core))):
        picked = jnp.dot(ref[...], picker, preferred_element_type=jnp.float32)
        source = lax.broadcasted_iota(jnp.int32, (ref.shape[0], WIN), 0)
        place = lax.broadcasted_iota(jnp.int32, (ref.shape[0], WIN), 1)
        shift = (source + start == place).astype(jnp.float32).astype(jnp.bfloat16)
        window = window + lax.dot_general(
            picked.astype(jnp.bfloat16),
            shift,
            (((0,), (0,)), ((), ())),
            preferred_element_type=jnp.float32,
        )
    window_ref[...] = window.astype(jnp.bfloat16)


def stack_kernel(window_ref, first_ref, second_ref, out_ref):
    core = lax.axis_index(CORE)

    @pl.when(core == 0)
    def _():
        out_ref[0] = window_ref[...]

    @pl.when(core != 0)
    def _():
        out_ref[0] = second_ref[...]

    out_ref[1] = first_ref[...]


def stage_kernel(integrals_ref, total_ref):
    del integrals_ref
    total_ref[...] = jnp.zeros_like(total_ref)


def half_kernel(parts, last, small_ref, integrals_ref, before_ref, *refs):
    *stack_refs, out_ref = refs
    slots, batch, _ = stack_refs[0].shape
    p_local, _, rows = integrals_ref.shape
    zh, zl, core = lax.axis_index(ZH), lax.axis_index(ZL), lax.axis_index(CORE)
    layers, width = lax.axis_size(ZH), lax.axis_size(X)
    near = jnp.where(zl == 0, layers - 1, 1)
    pairs = p_local // 2
    totals = [before_ref[pair] for pair in range(pairs)]
    masks = small_ref[...].astype(jnp.float32)
    entry = lax.broadcasted_iota(jnp.int32, masks.shape, 1)
    column = lax.broadcasted_iota(jnp.int32, (1, 2 * rows), 1) % rows
    for ref, (distance, mine) in zip(stack_refs, parts):
        x = lax.rem(lax.axis_index(X) + distance, width)
        holder = core if mine else 1 - core
        for slot in range(slots):
            even = 0 if slot == 0 else 2
            odd = layers - near if slot == 0 else near
            q = lax.rem(zh + jnp.where(holder == 0, even, odd), layers) * width + x
            offset = lax.rem(COL_BLK * q, ALIGN)
            chosen = jnp.sum(jnp.where(entry == q, masks, 0.0), axis=1, keepdims=True)
            keep = jnp.where(column < ROW_BLK, chosen[1:2, :], chosen[2:3, :])
            span = pl.ds(pl.multiple_of(COL_BLK * q - offset, ALIGN), WIN)
            for pair in range(pairs):
                block = jnp.concatenate(
                    [integrals_ref[2 * pair, span, :], integrals_ref[2 * pair + 1, span, :]],
                    axis=1,
                )
                product = jnp.dot(ref[slot], block, preferred_element_type=jnp.float32)
                totals[pair] = totals[pair] + product * keep
    if last:
        for p in range(p_local):
            part = totals[p // 2][:, (p % 2) * rows : (p % 2 + 1) * rows]
            out_ref[p * batch : (p + 1) * batch, :] = part.astype(jnp.bfloat16)
    else:
        for pair in range(pairs):
            out_ref[pair] = totals[pair]


def turned(index, size):
    return (index + size // 2) % size


def near_kernel(rows_dev, half_ref, previous_ref, left_ref, near_ref):
    rows = half_ref.shape[1]
    core = lax.axis_index(CORE)
    out_row = lax.broadcasted_iota(jnp.int32, (rows, rows), 0)
    in_row = lax.broadcasted_iota(jnp.int32, (rows, rows), 1)
    mine = out_row < rows // 2
    local = jnp.where(mine, out_row, out_row - rows // 2)
    parity = jnp.where(mine, core, 1 - core)
    place = local // rows_dev
    width = lax.axis_size(X)
    chip = turned(place // width, lax.axis_size(ZH)) * width + turned(place % width, width)
    wanted = chip * (2 * rows_dev) + parity * rows_dev + local % rows_dev
    order = (wanted == in_row).astype(jnp.float32).astype(jnp.bfloat16)
    left = lax.dot_general(
        order, half_ref[...], (((1,), (1,)), ((), ())), preferred_element_type=jnp.float32
    ).astype(jnp.bfloat16)
    left_ref[...] = left
    for j, ref in enumerate((half_ref, previous_ref)):
        near_ref[:, j * rows : (j + 1) * rows] = jnp.dot(
            left, ref[...], preferred_element_type=jnp.float32
        )


def band_kernel(left_ref, near_ref, farther_ref, own_ref, send_ref):
    rows = left_ref.shape[0]
    done = near_ref.shape[1]
    own_ref[:, :done] = near_ref[: rows // 2, :]
    send_ref[:, :done] = near_ref[rows // 2 :, :]
    product = jnp.dot(left_ref[...], farther_ref[...], preferred_element_type=jnp.float32)
    own_ref[:, done:] = product[: rows // 2]
    send_ref[:, done:] = product[rows // 2 :]


def from_behind(block, axis, distance):
    devices = range(lax.axis_size(axis))
    route = [((i - distance) % len(devices), i) for i in devices]
    return lax.ppermute(block, axis, route)


def along_z(block, steps):
    height, halves, cores = (lax.axis_size(a) for a in ((ZH, ZL), ZL, CORE))

    def place(z, core):
        return (z // halves * cores + core) * halves + z % halves

    route = [
        (place((z + steps[core, z % halves]) % height, core), place(z, core))
        for z in range(height)
        for core in range(cores)
        if (core, z % halves) in steps
    ]
    return lax.ppermute(block, (ZH, CORE, ZL), route)


def other_core(block):
    return lax.ppermute(block, CORE, [(0, 1), (1, 0)])


def params(mib):
    return pltpu.CompilerParams(vmem_limit_bytes=mib * MIB)


def per_device(integrals, block_mask, coefficients, occ_index):
    p_local, r_local, basis = integrals.shape
    cols = coefficients.shape[0]
    batch = occ_index.shape[0]
    chips = lax.axis_size((ZH, X))
    mask = block_mask[0]

    other_coefficients = other_core(coefficients)
    small = jnp.concatenate(
        [occ_index[None, :], jnp.pad(mask, ((0, 0), (0, batch - mask.shape[1])))], axis=0
    )
    padded = jnp.pad(coefficients, ((0, -cols % ALIGN), (0, 0)))
    window = pl.pallas_call(
        lambda *refs: pick_kernel(cols, *refs),
        out_shape=jax.ShapeDtypeStruct((batch, WIN), jnp.bfloat16),
        in_specs=[WHOLE] * 3,
        out_specs=WHOLE,
        compiler_params=params(4),
        name="pick",
    )(small, padded, other_coefficients)

    by_column = jnp.swapaxes(integrals, 1, 2)
    running = jax.ShapeDtypeStruct((p_local // 2, batch, 2 * r_local), jnp.float32)
    total = pl.pallas_call(
        stage_kernel,
        out_shape=running,
        in_specs=[pl.BlockSpec(memory_space=pl.ANY)],
        out_specs=WHOLE,
        compiler_params=params(52),
        name="stage",
    )(by_column)
    window, total = lax.optimization_barrier((window, total))
    second = along_z(window, {(1, 0): 2, (1, 1): -2})
    first = along_z(window, {(0, 0): -3, (0, 1): 3, (1, 0): -1, (1, 1): 1})
    first, window = lax.optimization_barrier((first, window))
    stack = pl.pallas_call(
        stack_kernel,
        out_shape=jax.ShapeDtypeStruct((2, batch, WIN), jnp.bfloat16),
        in_specs=[WHOLE] * 3,
        out_specs=WHOLE,
        compiler_params=params(4),
        name="stack",
    )(window, first, second)

    def add_products(total, parts, stacks, last=False, cost=None):
        out = jax.ShapeDtypeStruct((p_local * batch, r_local), jnp.bfloat16) if last else running
        return pl.pallas_call(
            lambda *refs: half_kernel(parts, last, *refs),
            out_shape=out,
            in_specs=[WHOLE] * (3 + len(stacks)),
            out_specs=WHOLE,
            compiler_params=params(12),
            cost_estimate=cost
            or pl.CostEstimate(
                flops=2 * batch * WIN * 2 * len(stacks) * p_local * r_local,
                bytes_accessed=by_column.size * len(stacks) // 4,
                transcendentals=0,
            ),
            name="half",
        )(small, by_column, total, *stacks)

    brief = pl.CostEstimate(flops=1, bytes_accessed=4096, transcendentals=0)
    total = add_products(total, [(0, True)], [stack], cost=brief)
    parts, stacks = [(0, False)], [other_core(stack)]
    for distance in (2, 1, 3):
        own = from_behind(stack, X, -distance)
        if distance == 2:
            own, total = lax.optimization_barrier((own, total))
        parts += [(distance, True), (distance, False)]
        stacks += [own, other_core(own)]
        total = add_products(total, parts, stacks, last=distance == 3)
        parts, stacks = [], []
    half = total

    previous = from_behind(half, ROW, 1)
    farther = from_behind(half, ROW, 2)
    rows_dev = r_local // (chips * lax.axis_size(CORE))
    left, near = pl.pallas_call(
        lambda *refs: near_kernel(rows_dev, *refs),
        out_shape=(
            jax.ShapeDtypeStruct(half.shape[::-1], jnp.bfloat16),
            jax.ShapeDtypeStruct((r_local, (BANDS - 1) * r_local), jnp.float32),
        ),
        in_specs=[WHOLE] * 2,
        out_specs=(WHOLE, WHOLE),
        compiler_params=params(4),
        cost_estimate=pl.CostEstimate(flops=1, bytes_accessed=4096, transcendentals=0),
        name="near",
    )(half, previous)
    part = jax.ShapeDtypeStruct((chips * rows_dev, BANDS * r_local), jnp.float32)
    kept, sent = pl.pallas_call(
        band_kernel,
        out_shape=(part, part),
        in_specs=[WHOLE] * 3,
        out_specs=(WHOLE, WHOLE),
        compiler_params=params(4),
        name="bands",
    )(left, near, farther)
    chip_sum = kept + other_core(sent)
    layers, width = lax.axis_size(ZH), lax.axis_size(X)
    order = [
        turned(zh, layers) * width + turned(x, width) for zh in range(layers) for x in range(width)
    ]
    pieces = lax.all_to_all(
        chip_sum.reshape(chips, rows_dev, BANDS * r_local),
        (ZH, X),
        0,
        0,
        axis_index_groups=[order],
    )
    return jnp.sum(pieces, axis=0)


def solution(mesh):
    fine = Mesh(mesh.devices.reshape(4, 4, 2, 2, 4), AUX + ROW)
    in_specs = (P(AUX, ROW, None), P(AUX, ROW, None), P(AUX, None), P())
    out_specs = P(ROW + AUX, None)
    return jax.shard_map(
        per_device, mesh=fine, in_specs=in_specs, out_specs=out_specs, check_vma=False
    )
```

```python
import jax
import jax.numpy as jnp
from jax import lax
from jax.experimental import pallas as pl
from jax.experimental.pallas import tpu as pltpu
from jax.sharding import Mesh, PartitionSpec as P

BANDS = 3
COL_BLK = 500
WIN = 512
ALIGN = 16
ROW_BLK = 64
MIB = 1024 * 1024

ZH, X, CORE, ZL, Y = "zh", "x", "core", "zl", "y"
AUX = (ZH, X, CORE)
ROW = (ZL, Y)


WHOLE = pl.BlockSpec(memory_space=pltpu.VMEM)


def window_offset(q):
    return (COL_BLK * q) % ALIGN


def pick_kernel(cols, small_ref, own_ref, other_ref, window_ref):
    batch = small_ref.shape[1]
    chip = lax.axis_index(ZH) * lax.axis_size(X) + lax.axis_index(X)
    core = lax.axis_index(CORE)
    offset = window_offset(chip)
    picker = lax.broadcasted_iota(jnp.int32, (own_ref.shape[1], batch), 0) == small_ref[0:1, :]
    picker = picker.astype(jnp.float32).astype(jnp.bfloat16)
    window = jnp.zeros((batch, WIN), jnp.float32)
    for ref, start in ((own_ref, offset + cols * core), (other_ref, offset + cols * (1 - core))):
        picked = jnp.dot(ref[...], picker, preferred_element_type=jnp.float32)
        source = lax.broadcasted_iota(jnp.int32, (ref.shape[0], WIN), 0)
        place = lax.broadcasted_iota(jnp.int32, (ref.shape[0], WIN), 1)
        shift = (source + start == place).astype(jnp.float32).astype(jnp.bfloat16)
        window = window + lax.dot_general(
            picked.astype(jnp.bfloat16),
            shift,
            (((0,), (0,)), ((), ())),
            preferred_element_type=jnp.float32,
        )
    window_ref[...] = window.astype(jnp.bfloat16)


def stack_kernel(window_ref, first_ref, second_ref, out_ref):
    core = lax.axis_index(CORE)

    @pl.when(core == 0)
    def _():
        out_ref[0] = window_ref[...]

    @pl.when(core != 0)
    def _():
        out_ref[0] = second_ref[...]

    out_ref[1] = first_ref[...]


def stage_kernel(integrals_ref, token_ref):
    del integrals_ref
    token_ref[...] = jnp.zeros_like(token_ref)


def half_kernel(parts, last, small_ref, integrals_ref, before_ref, *refs):
    *stack_refs, out_ref = refs
    slots, batch, _ = stack_refs[0].shape
    p_local, _, rows = integrals_ref.shape
    zh, zl, core = lax.axis_index(ZH), lax.axis_index(ZL), lax.axis_index(CORE)
    layers, width = lax.axis_size(ZH), lax.axis_size(X)
    near = jnp.where(zl == 0, layers - 1, 1)
    pairs = p_local // 2
    if before_ref.shape[0] == pairs:
        totals = [before_ref[pair] for pair in range(pairs)]
    else:
        totals = [jnp.zeros((batch, 2 * rows), jnp.float32) + before_ref[0:1, 0:1]] * pairs
    masks = small_ref[...].astype(jnp.float32)
    entry = lax.broadcasted_iota(jnp.int32, masks.shape, 1)
    column = lax.broadcasted_iota(jnp.int32, (1, 2 * rows), 1) % rows
    for ref, (distance, mine) in zip(stack_refs, parts):
        x = lax.rem(lax.axis_index(X) + distance, width)
        holder = core if mine else 1 - core
        for slot in range(slots):
            even = 0 if slot == 0 else 2
            odd = near if slot == 0 else layers - near
            q = lax.rem(zh + jnp.where(holder == 0, even, odd), layers) * width + x
            offset = lax.rem(COL_BLK * q, ALIGN)
            chosen = jnp.sum(jnp.where(entry == q, masks, 0.0), axis=1, keepdims=True)
            keep = jnp.where(column < ROW_BLK, chosen[1:2, :], chosen[2:3, :])
            span = pl.ds(pl.multiple_of(COL_BLK * q - offset, ALIGN), WIN)
            for pair in range(pairs):
                block = jnp.concatenate(
                    [integrals_ref[2 * pair, span, :], integrals_ref[2 * pair + 1, span, :]],
                    axis=1,
                )
                product = jnp.dot(ref[slot], block, preferred_element_type=jnp.float32)
                totals[pair] = totals[pair] + product * keep
    if last:
        for p in range(p_local):
            part = totals[p // 2][:, (p % 2) * rows : (p % 2 + 1) * rows]
            out_ref[p * batch : (p + 1) * batch, :] = part.astype(jnp.bfloat16)
    else:
        for pair in range(pairs):
            out_ref[pair] = totals[pair]


def turned(index, size):
    return (index + size // 2) % size


def near_kernel(rows_dev, half_ref, previous_ref, left_ref, near_ref):
    rows = half_ref.shape[1]
    core = lax.axis_index(CORE)
    out_row = lax.broadcasted_iota(jnp.int32, (rows, rows), 0)
    in_row = lax.broadcasted_iota(jnp.int32, (rows, rows), 1)
    mine = out_row < rows // 2
    local = jnp.where(mine, out_row, out_row - rows // 2)
    parity = jnp.where(mine, core, 1 - core)
    place = local // rows_dev
    width = lax.axis_size(X)
    chip = turned(place // width, lax.axis_size(ZH)) * width + turned(place % width, width)
    wanted = chip * (2 * rows_dev) + parity * rows_dev + local % rows_dev
    order = (wanted == in_row).astype(jnp.float32).astype(jnp.bfloat16)
    left = lax.dot_general(
        order, half_ref[...], (((1,), (1,)), ((), ())), preferred_element_type=jnp.float32
    ).astype(jnp.bfloat16)
    left_ref[...] = left
    for j, ref in enumerate((half_ref, previous_ref)):
        near_ref[:, j * rows : (j + 1) * rows] = jnp.dot(
            left, ref[...], preferred_element_type=jnp.float32
        )


def band_kernel(left_ref, near_ref, farther_ref, own_ref, send_ref):
    rows = left_ref.shape[0]
    done = near_ref.shape[1]
    own_ref[:, :done] = near_ref[: rows // 2, :]
    send_ref[:, :done] = near_ref[rows // 2 :, :]
    product = jnp.dot(left_ref[...], farther_ref[...], preferred_element_type=jnp.float32)
    own_ref[:, done:] = product[: rows // 2]
    send_ref[:, done:] = product[rows // 2 :]


def from_behind(block, axis, distance):
    devices = range(lax.axis_size(axis))
    route = [((i - distance) % len(devices), i) for i in devices]
    return lax.ppermute(block, axis, route)


def along_z(block, steps):
    height, halves, cores = (lax.axis_size(a) for a in ((ZH, ZL), ZL, CORE))

    def place(z, core):
        return (z // halves * cores + core) * halves + z % halves

    route = [
        (place((z + steps[core, z % halves]) % height, core), place(z, core))
        for z in range(height)
        for core in range(cores)
        if (core, z % halves) in steps
    ]
    return lax.ppermute(block, (ZH, CORE, ZL), route)


def other_core(block):
    return lax.ppermute(block, CORE, [(0, 1), (1, 0)])


def params(mib):
    return pltpu.CompilerParams(vmem_limit_bytes=mib * MIB)


def per_device(integrals, block_mask, coefficients, occ_index):
    p_local, r_local, basis = integrals.shape
    cols = coefficients.shape[0]
    batch = occ_index.shape[0]
    chips = lax.axis_size((ZH, X))
    mask = block_mask[0]

    other_coefficients = other_core(coefficients)
    small = jnp.concatenate(
        [occ_index[None, :], jnp.pad(mask, ((0, 0), (0, batch - mask.shape[1])))], axis=0
    )
    padded = jnp.pad(coefficients, ((0, -cols % ALIGN), (0, 0)))
    window = pl.pallas_call(
        lambda *refs: pick_kernel(cols, *refs),
        out_shape=jax.ShapeDtypeStruct((batch, WIN), jnp.bfloat16),
        in_specs=[WHOLE] * 3,
        out_specs=WHOLE,
        compiler_params=params(4),
        name="pick",
    )(small, padded, other_coefficients)

    by_column = jnp.swapaxes(integrals, 1, 2)
    running = jax.ShapeDtypeStruct((p_local // 2, batch, 2 * r_local), jnp.float32)
    total = pl.pallas_call(
        stage_kernel,
        out_shape=jax.ShapeDtypeStruct((8, 128), jnp.float32),
        in_specs=[pl.BlockSpec(memory_space=pl.ANY)],
        out_specs=WHOLE,
        compiler_params=params(52),
        name="stage",
    )(by_column)
    window, total = lax.optimization_barrier((window, total))
    second = along_z(window, {(1, 0): -1, (1, 1): 1})
    first = along_z(window, {(0, 0): -3, (0, 1): 3, (1, 0): 2, (1, 1): -2})
    first, window = lax.optimization_barrier((first, window))
    stack = pl.pallas_call(
        stack_kernel,
        out_shape=jax.ShapeDtypeStruct((2, batch, WIN), jnp.bfloat16),
        in_specs=[WHOLE] * 3,
        out_specs=WHOLE,
        compiler_params=params(4),
        name="stack",
    )(window, first, second)

    def add_products(total, parts, stacks, last=False, cost=None):
        out = jax.ShapeDtypeStruct((p_local * batch, r_local), jnp.bfloat16) if last else running
        return pl.pallas_call(
            lambda *refs: half_kernel(parts, last, *refs),
            out_shape=out,
            in_specs=[WHOLE] * (3 + len(stacks)),
            out_specs=WHOLE,
            compiler_params=params(12),
            cost_estimate=cost
            or pl.CostEstimate(
                flops=2 * batch * WIN * 2 * len(stacks) * p_local * r_local,
                bytes_accessed=by_column.size * len(stacks) // 4,
                transcendentals=0,
            ),
            name="half",
        )(small, by_column, total, *stacks)

    brief = pl.CostEstimate(flops=1, bytes_accessed=4096, transcendentals=0)
    total = add_products(total, [(0, True)], [stack], cost=brief)
    parts, stacks = [(0, False)], [other_core(stack)]
    for distance in (2, 1, 3):
        own = from_behind(stack, X, -distance)
        if distance == 2:
            own, total = lax.optimization_barrier((own, total))
        parts += [(distance, True), (distance, False)]
        stacks += [own, other_core(own)]
        total = add_products(total, parts, stacks, last=distance == 3)
        parts, stacks = [], []
    half = total

    previous = from_behind(half, ROW, 1)
    farther = from_behind(half, ROW, 2)
    rows_dev = r_local // (chips * lax.axis_size(CORE))
    left, near = pl.pallas_call(
        lambda *refs: near_kernel(rows_dev, *refs),
        out_shape=(
            jax.ShapeDtypeStruct(half.shape[::-1], jnp.bfloat16),
            jax.ShapeDtypeStruct((r_local, (BANDS - 1) * r_local), jnp.float32),
        ),
        in_specs=[WHOLE] * 2,
        out_specs=(WHOLE, WHOLE),
        compiler_params=params(4),
        cost_estimate=pl.CostEstimate(flops=1, bytes_accessed=4096, transcendentals=0),
        name="near",
    )(half, previous)
    part = jax.ShapeDtypeStruct((chips * rows_dev, BANDS * r_local), jnp.float32)
    kept, sent = pl.pallas_call(
        band_kernel,
        out_shape=(part, part),
        in_specs=[WHOLE] * 3,
        out_specs=(WHOLE, WHOLE),
        compiler_params=params(4),
        name="bands",
    )(left, near, farther)
    chip_sum = kept + other_core(sent)
    layers, width = lax.axis_size(ZH), lax.axis_size(X)
    order = [
        turned(zh, layers) * width + turned(x, width) for zh in range(layers) for x in range(width)
    ]
    pieces = lax.all_to_all(
        chip_sum.reshape(chips, rows_dev, BANDS * r_local),
        (ZH, X),
        0,
        0,
        axis_index_groups=[order],
    )
    return jnp.sum(pieces, axis=0)


def solution(mesh):
    fine = Mesh(mesh.devices.reshape(4, 4, 2, 2, 4), AUX + ROW)
    in_specs = (P(AUX, ROW, None), P(AUX, ROW, None), P(AUX, None), P())
    out_specs = P(ROW + AUX, None)
    return jax.shard_map(
        per_device, mesh=fine, in_specs=in_specs, out_specs=out_specs, check_vma=False
    )
```

```python
import jax
import jax.numpy as jnp
from jax import lax
from jax.experimental import pallas as pl
from jax.experimental.pallas import tpu as pltpu
from jax.sharding import Mesh, PartitionSpec as P

BANDS = 3
COL_BLK = 500
WIN = 512
ALIGN = 16
ROW_BLK = 64
MIB = 1024 * 1024

ZH, X, CORE, ZL, Y = "zh", "x", "core", "zl", "y"
AUX = (ZH, X, CORE)
ROW = (ZL, Y)


WHOLE = pl.BlockSpec(memory_space=pltpu.VMEM)


def window_offset(q):
    return (COL_BLK * q) % ALIGN


def pick_kernel(cols, small_ref, own_ref, other_ref, window_ref):
    batch = small_ref.shape[1]
    chip = lax.axis_index(ZH) * lax.axis_size(X) + lax.axis_index(X)
    core = lax.axis_index(CORE)
    offset = window_offset(chip)
    picker = lax.broadcasted_iota(jnp.int32, (own_ref.shape[1], batch), 0) == small_ref[0:1, :]
    picker = picker.astype(jnp.float32).astype(jnp.bfloat16)
    window = jnp.zeros((batch, WIN), jnp.float32)
    for ref, start in ((own_ref, offset + cols * core), (other_ref, offset + cols * (1 - core))):
        picked = jnp.dot(ref[...], picker, preferred_element_type=jnp.float32)
        source = lax.broadcasted_iota(jnp.int32, (ref.shape[0], WIN), 0)
        place = lax.broadcasted_iota(jnp.int32, (ref.shape[0], WIN), 1)
        shift = (source + start == place).astype(jnp.float32).astype(jnp.bfloat16)
        window = window + lax.dot_general(
            picked.astype(jnp.bfloat16),
            shift,
            (((0,), (0,)), ((), ())),
            preferred_element_type=jnp.float32,
        )
    window_ref[...] = window.astype(jnp.bfloat16)


def stack_kernel(window_ref, first_ref, second_ref, out_ref):
    core = lax.axis_index(CORE)

    @pl.when(core == 0)
    def _():
        out_ref[0] = window_ref[...]

    @pl.when(core != 0)
    def _():
        out_ref[0] = second_ref[...]

    out_ref[1] = first_ref[...]


def stage_kernel(integrals_ref, token_ref):
    del integrals_ref
    token_ref[...] = jnp.zeros_like(token_ref)


def half_kernel(parts, last, small_ref, integrals_ref, before_ref, *refs):
    *stack_refs, out_ref = refs
    slots, batch, _ = stack_refs[0].shape
    p_local, _, rows = integrals_ref.shape
    zh, zl, core = lax.axis_index(ZH), lax.axis_index(ZL), lax.axis_index(CORE)
    layers, width = lax.axis_size(ZH), lax.axis_size(X)
    near = jnp.where(zl == 0, layers - 1, 1)
    pairs = p_local // 2
    if before_ref.shape[0] == pairs:
        totals = [before_ref[pair] for pair in range(pairs)]
    else:
        totals = [jnp.zeros((batch, 2 * rows), jnp.float32) + before_ref[0:1, 0:1]] * pairs
    masks = small_ref[...].astype(jnp.float32)
    entry = lax.broadcasted_iota(jnp.int32, masks.shape, 1)
    column = lax.broadcasted_iota(jnp.int32, (1, 2 * rows), 1) % rows
    for ref, (distance, mine) in zip(stack_refs, parts):
        x = lax.rem(lax.axis_index(X) + distance, width)
        holder = core if mine else 1 - core
        for slot in range(slots):
            even = 0 if slot == 0 else 2
            odd = near if slot == 0 else layers - near
            q = lax.rem(zh + jnp.where(holder == 0, even, odd), layers) * width + x
            offset = lax.rem(COL_BLK * q, ALIGN)
            chosen = jnp.sum(jnp.where(entry == q, masks, 0.0), axis=1, keepdims=True)
            keep = jnp.where(column < ROW_BLK, chosen[1:2, :], chosen[2:3, :])
            span = pl.ds(pl.multiple_of(COL_BLK * q - offset, ALIGN), WIN)
            for pair in range(pairs):
                block = jnp.concatenate(
                    [integrals_ref[2 * pair, span, :], integrals_ref[2 * pair + 1, span, :]],
                    axis=1,
                )
                product = jnp.dot(ref[slot], block, preferred_element_type=jnp.float32)
                totals[pair] = totals[pair] + product * keep
    if last:
        for p in range(p_local):
            part = totals[p // 2][:, (p % 2) * rows : (p % 2 + 1) * rows]
            out_ref[p * batch : (p + 1) * batch, :] = part.astype(jnp.bfloat16)
    else:
        for pair in range(pairs):
            out_ref[pair] = totals[pair]


def turned(index, size):
    return (index + size // 2) % size


def near_kernel(rows_dev, half_ref, previous_ref, left_ref, near_ref):
    rows = half_ref.shape[1]
    core = lax.axis_index(CORE)
    out_row = lax.broadcasted_iota(jnp.int32, (rows, rows), 0)
    in_row = lax.broadcasted_iota(jnp.int32, (rows, rows), 1)
    mine = out_row < rows // 2
    local = jnp.where(mine, out_row, out_row - rows // 2)
    parity = jnp.where(mine, core, 1 - core)
    place = local // rows_dev
    width = lax.axis_size(X)
    chip = turned(place // width, lax.axis_size(ZH)) * width + turned(place % width, width)
    wanted = chip * (2 * rows_dev) + parity * rows_dev + local % rows_dev
    order = (wanted == in_row).astype(jnp.float32).astype(jnp.bfloat16)
    left = lax.dot_general(
        order, half_ref[...], (((1,), (1,)), ((), ())), preferred_element_type=jnp.float32
    ).astype(jnp.bfloat16)
    left_ref[...] = left
    for j, ref in enumerate((half_ref, previous_ref)):
        near_ref[:, j * rows : (j + 1) * rows] = jnp.dot(
            left, ref[...], preferred_element_type=jnp.float32
        )


def band_kernel(left_ref, near_ref, farther_ref, own_ref, send_ref):
    rows = left_ref.shape[0]
    done = near_ref.shape[1]
    own_ref[:, :done] = near_ref[: rows // 2, :]
    send_ref[:, :done] = near_ref[rows // 2 :, :]
    product = jnp.dot(left_ref[...], farther_ref[...], preferred_element_type=jnp.float32)
    own_ref[:, done:] = product[: rows // 2]
    send_ref[:, done:] = product[rows // 2 :]


def from_behind(block, axis, distance):
    devices = range(lax.axis_size(axis))
    route = [((i - distance) % len(devices), i) for i in devices]
    return lax.ppermute(block, axis, route)


def along_z(block, steps):
    height, halves, cores = (lax.axis_size(a) for a in ((ZH, ZL), ZL, CORE))

    def place(z, core):
        return (z // halves * cores + core) * halves + z % halves

    route = [
        (place((z + steps[core, z % halves]) % height, core), place(z, core))
        for z in range(height)
        for core in range(cores)
        if (core, z % halves) in steps
    ]
    return lax.ppermute(block, (ZH, CORE, ZL), route)


def other_core(block):
    return lax.ppermute(block, CORE, [(0, 1), (1, 0)])


def params(mib):
    return pltpu.CompilerParams(vmem_limit_bytes=mib * MIB)


def per_device(integrals, block_mask, coefficients, occ_index):
    p_local, r_local, basis = integrals.shape
    cols = coefficients.shape[0]
    batch = occ_index.shape[0]
    chips = lax.axis_size((ZH, X))
    mask = block_mask[0]

    other_coefficients = other_core(coefficients)
    small = jnp.concatenate(
        [occ_index[None, :], jnp.pad(mask, ((0, 0), (0, batch - mask.shape[1])))], axis=0
    )
    padded = jnp.pad(coefficients, ((0, -cols % ALIGN), (0, 0)))
    window = pl.pallas_call(
        lambda *refs: pick_kernel(cols, *refs),
        out_shape=jax.ShapeDtypeStruct((batch, WIN), jnp.bfloat16),
        in_specs=[WHOLE] * 3,
        out_specs=WHOLE,
        compiler_params=params(4),
        name="pick",
    )(small, padded, other_coefficients)

    by_column = jnp.swapaxes(integrals, 1, 2)
    running = jax.ShapeDtypeStruct((p_local // 2, batch, 2 * r_local), jnp.float32)
    total = pl.pallas_call(
        stage_kernel,
        out_shape=jax.ShapeDtypeStruct((8, 128), jnp.float32),
        in_specs=[pl.BlockSpec(memory_space=pl.ANY)],
        out_specs=WHOLE,
        compiler_params=params(52),
        name="stage",
    )(by_column)
    window, total = lax.optimization_barrier((window, total))
    second = along_z(window, {(1, 0): -1, (1, 1): 1})
    first = along_z(window, {(0, 0): -3, (0, 1): 3, (1, 0): 2, (1, 1): -2})
    first, window = lax.optimization_barrier((first, window))
    stack = pl.pallas_call(
        stack_kernel,
        out_shape=jax.ShapeDtypeStruct((2, batch, WIN), jnp.bfloat16),
        in_specs=[WHOLE] * 3,
        out_specs=WHOLE,
        compiler_params=params(4),
        name="stack",
    )(window, first, second)

    def add_products(total, parts, stacks, last=False, cost=None):
        out = jax.ShapeDtypeStruct((p_local * batch, r_local), jnp.bfloat16) if last else running
        return pl.pallas_call(
            lambda *refs: half_kernel(parts, last, *refs),
            out_shape=out,
            in_specs=[WHOLE] * (3 + len(stacks)),
            out_specs=WHOLE,
            compiler_params=params(12),
            cost_estimate=cost
            or pl.CostEstimate(
                flops=2 * batch * WIN * 2 * len(stacks) * p_local * r_local,
                bytes_accessed=by_column.size * len(stacks) // 4,
                transcendentals=0,
            ),
            name="half",
        )(small, by_column, total, *stacks)

    brief = pl.CostEstimate(flops=1, bytes_accessed=4096, transcendentals=0)
    total = add_products(total, [(0, True)], [stack], cost=brief)
    parts, stacks = [(0, False)], [other_core(stack)]
    for distance in (2, 1, 3):
        own = from_behind(stack, X, -distance)
        if distance == 2:
            own, total = lax.optimization_barrier((own, total))
        if distance == 3:
            total = add_products(total, [(distance, True)], [own])
            total = add_products(total, [(distance, False)], [other_core(own)], last=True)
        else:
            parts += [(distance, True), (distance, False)]
            stacks += [own, other_core(own)]
            total = add_products(total, parts, stacks)
        parts, stacks = [], []
    half = total

    previous = from_behind(half, ROW, 1)
    farther = from_behind(half, ROW, 2)
    rows_dev = r_local // (chips * lax.axis_size(CORE))
    left, near = pl.pallas_call(
        lambda *refs: near_kernel(rows_dev, *refs),
        out_shape=(
            jax.ShapeDtypeStruct(half.shape[::-1], jnp.bfloat16),
            jax.ShapeDtypeStruct((r_local, (BANDS - 1) * r_local), jnp.float32),
        ),
        in_specs=[WHOLE] * 2,
        out_specs=(WHOLE, WHOLE),
        compiler_params=params(4),
        cost_estimate=pl.CostEstimate(flops=1, bytes_accessed=4096, transcendentals=0),
        name="near",
    )(half, previous)
    part = jax.ShapeDtypeStruct((chips * rows_dev, BANDS * r_local), jnp.float32)
    kept, sent = pl.pallas_call(
        band_kernel,
        out_shape=(part, part),
        in_specs=[WHOLE] * 3,
        out_specs=(WHOLE, WHOLE),
        compiler_params=params(4),
        name="bands",
    )(left, near, farther)
    chip_sum = kept + other_core(sent)
    layers, width = lax.axis_size(ZH), lax.axis_size(X)
    order = [
        turned(zh, layers) * width + turned(x, width) for zh in range(layers) for x in range(width)
    ]
    pieces = lax.all_to_all(
        chip_sum.reshape(chips, rows_dev, BANDS * r_local),
        (ZH, X),
        0,
        0,
        axis_index_groups=[order],
    )
    return jnp.sum(pieces, axis=0)


def solution(mesh):
    fine = Mesh(mesh.devices.reshape(4, 4, 2, 2, 4), AUX + ROW)
    in_specs = (P(AUX, ROW, None), P(AUX, ROW, None), P(AUX, None), P())
    out_specs = P(ROW + AUX, None)
    return jax.shard_map(
        per_device, mesh=fine, in_specs=in_specs, out_specs=out_specs, check_vma=False
    )
```
